256 devices in a mesh: row: 8 (over y_lo, x), col: 32 (over z, y_hi, core).
Axes of the slice: x: 4, y: 4 (y_hi: 2, y_lo: 2; y = y_hi * 2 + y_lo), z: 8, core: 2. Of those that a mesh axis runs over, the one named last changes fastest.
Arguments:
- amplitudes: bfloat16 [800, 640000], P('col', 'row'), may hold values from -6 to 6
- singles: bfloat16 [100, 800], P(None, 'col'), may hold values from -3 to 3
- integrals: bfloat16 [800, 1280000], P('col', 'row'), may hold values from -0.01953125 to 0.01953125
- virt_irrep: int32 [32], replicated, may hold values from 0 to 7
- occ_irrep: int32 [100], replicated, may hold values from 0 to 7
Outputs:
- ladder: bfloat16 [800, 2, 800], P('row', None, 'col')
The draws below stay inside these ranges and needn't reach their ends.
Inputs may be any that keep to these rules, and one draw needn't show every extreme that they name: `virt_irrep`: irreps of the point group. `occ_irrep`: irreps of the point group.
All inputs are finite; a program needn't handle non-finite values.
Results may differ from the reference program's by a relative error of at most 0.0049.
Values may be sent and summed in bfloat16 or wider, within the bound.
A program may use at most 128 MiB of HBM per device.

```python
import jax
import jax.numpy as jnp
from jax import lax

NV = 800
NOCC = 100
VB = 25
PANEL = 2
PI = 8
NBLK = 32
PAIRS = 800


def set_ends(drawn, own_key, low, high):
    extent = drawn.shape
    place = [jax.random.randint(jax.random.fold_in(own_key, axis), (), 0, extent[axis]) for axis in range(len(extent))]
    drawn = drawn.at[tuple(place)].set(low)
    longest = extent.index(max(extent))
    place[longest] = (place[longest] + 1) % extent[longest]
    return drawn.at[tuple(place)].set(high)


def block_scale(own_key, extent, pieces, smallest, top_value):
    gain, own = 1.0, jax.random.fold_in(own_key, 6)
    for dim, shards_of in pieces:
        steps = jnp.exp(jax.random.uniform(jax.random.fold_in(own, dim), (shards_of,), jnp.float32, smallest / len(pieces), top_value / len(pieces)))
        gain = gain * jnp.repeat(steps, extent[dim] // shards_of).reshape([-1 if axis == dim else 1 for axis in range(len(extent))])
    return gain


def normal_values(key, dims, deviation, most, shards=(), held_as=jnp.bfloat16):
    result = deviation * jax.random.normal(key, dims, jnp.float32)
    if shards:
        result = result * block_scale(key, dims, shards, -0.22, 0.18)
    return jnp.clip(result, -most, most).astype(held_as)


def setup_inputs(seed: int = 0) -> dict:
    streams_of = jax.random.split(jax.random.key(seed), 6)
    return {
        "amplitudes": normal_values(streams_of[0], (NV, NV * PAIRS), 1.0, 6.0, ((0, 32), (1, 8))),
        "singles": normal_values(streams_of[1], (NOCC, NV), 0.5, 3.0, ((1, 32),)),
        "integrals": normal_values(streams_of[2], (NV, NV * PANEL * NV), (NV * NV // 8) ** -0.5, 0.01953125, ((0, 32), (1, 8))),
        "virt_irrep": set_ends(jax.random.randint(streams_of[3], (NBLK,), 0, 8), jax.random.fold_in(streams_of[3], 1), 0, 7).astype(jnp.int32),
        "occ_irrep": set_ends(jax.random.randint(streams_of[4], (NOCC,), 0, 8), jax.random.fold_in(streams_of[4], 1), 0, 7).astype(jnp.int32),
    }


def reference(amplitudes, singles, integrals, virt_irrep, occ_irrep):
    orbital_irrep = jnp.repeat(virt_irrep, VB, total_repeat_length=NV)
    pair_irrep = jnp.bitwise_xor(occ_irrep[:PI][:, None], occ_irrep[None, :]).reshape(PAIRS)
    panel_irrep = orbital_irrep[:PANEL]
    outer_irrep = jnp.bitwise_xor(panel_irrep[:, None], orbital_irrep[None, :]).reshape(PANEL * NV)
    singles_i = singles[:PI].astype(jnp.float32)
    singles_d = jnp.transpose(singles.astype(jnp.float32))
    amp_three = amplitudes.reshape(NV, NV, PAIRS)
    int_three = integrals.reshape(NV, NV, PANEL * NV)

    def add_block(running, block_index):
        start = (block_index * VB).astype(jnp.int32)
        zero = jnp.int32(0)
        amp_block = lax.dynamic_slice(amp_three, (zero, start, zero), (NV, VB, PAIRS))
        block_irrep = lax.dynamic_slice(orbital_irrep, (start,), (VB,))
        first_single = lax.dynamic_slice(singles_i, (zero, start), (PI, VB))
        outer_part = (singles_d[:, None, None, :] * jnp.transpose(first_single)[None, :, :, None]).reshape(NV, VB, PAIRS)
        allowed = jnp.bitwise_xor(jnp.bitwise_xor(orbital_irrep[:, None, None], block_irrep[None, :, None]), pair_irrep[None, None, :]) == 0
        combined = jnp.where(allowed, amp_block.astype(jnp.float32) + outer_part, 0.0).astype(jnp.bfloat16)
        int_block = lax.dynamic_slice(int_three, (zero, start, zero), (NV, VB, PANEL * NV))
        int_allowed = jnp.bitwise_xor(jnp.bitwise_xor(orbital_irrep[:, None, None], block_irrep[None, :, None]), outer_irrep[None, None, :]) == 0
        blocked = jnp.where(int_allowed, int_block, jnp.zeros((), jnp.bfloat16))
        term = lax.dot_general(combined.reshape(NV * VB, PAIRS), blocked.reshape(NV * VB, PANEL * NV), (((0,), (0,)), ((), ())), preferred_element_type=jnp.float32)
        return running + term, None

    running = jnp.zeros((PAIRS, PANEL * NV), jnp.float32)
    running, unused = lax.scan(add_block, running, jnp.arange(NBLK, dtype=jnp.int32))
    return running.reshape(PAIRS, PANEL, NV).astype(jnp.bfloat16)
```

```python
import functools

import jax
import jax.numpy as jnp
from jax import lax
from jax.experimental import pallas as pl
from jax.experimental.pallas import tpu as pltpu
from jax.sharding import PartitionSpec as P

MESH = pl.DeviceIdType.MESH
BF = jnp.bfloat16
F32 = jnp.float32
I32 = jnp.int32

VB = 25
NB = 32
NOCC = 100
PI = 8
NV = 800
ROWS, COLS = 8, 32
NC = 100
SLOT = 32
WIN = 896
ALEN = 157 * 128
KP = 1792
TILES = ((0, 256), (256, 256), (512, 256), (768, 128))


def iota(shape, dim):
    return lax.broadcasted_iota(I32, shape, dim)


def pad_rows(x):
    return jnp.concatenate([x, jnp.zeros((32 - x.shape[0], x.shape[1]), x.dtype)], axis=0)


def kernel(
    round_ref, virt, occ, occ_row, singles, amp, integ,
    out, rounds_out,
    av, bv, enc, onehot, cs, ct, masks, acc, sj, sc, s_own, s_in, expand,
    core_out, core_in, qf, qb, row_in, wsum, zb, zf, col_in, res,
    asem, bsem, ssend, srecv, csend, crecv, rsend, rrecv, zsend, zrecv,
):
    r = lax.axis_index("row")
    c = lax.axis_index("col")
    core = lax.rem(c, 2)
    partner = c + 1 - 2 * core

    def amp_copy(q):
        return pltpu.make_async_copy(
            amp.at[:, pl.ds(q * (156 * 128), ALEN)], av.at[q], asem.at[q]
        )

    for q in range(4):
        amp_copy(q).start()

    def int_copy(a, k):
        src = pl.multiple_of(128 * ((25 * k - lax.rem(k, 2)) // 2 + 6 * a), 128)
        dst = pl.multiple_of(k * WIN, 128)
        return pltpu.make_async_copy(
            integ.at[:, pl.ds(src, WIN)], bv.at[a, :, pl.ds(dst, WIN)], bsem.at[a]
        )

    for a in range(2):
        def start_int(k, carry, a=a):
            int_copy(a, k).start()
            return carry
        lax.fori_loop(0, NC, start_int, 0)

    barrier = pltpu.get_barrier_semaphore()
    mate_row = c // 4
    far = r != mate_row

    def greet_col(k, carry):
        pl.semaphore_signal(
            barrier, inc=1, device_id=(r, lax.rem(c + k, COLS)), device_id_type=MESH
        )
        return carry

    lax.fori_loop(1, COLS, greet_col, 0)

    def greet_row(k, carry):
        pl.semaphore_signal(
            barrier, inc=1, device_id=(lax.rem(r + k, ROWS), c), device_id_type=MESH
        )
        return carry

    lax.fori_loop(1, ROWS, greet_row, 0)

    @pl.when(far)
    def _():
        for q in range(4):
            pl.semaphore_signal(
                barrier, inc=1, device_id=(mate_row, 4 * r + q), device_id_type=MESH
            )

    first_rank = round_ref[0] * SLOT
    lane = iota((128, 128), 1)
    sub = iota((128, 128), 0)
    h_row = jnp.concatenate([occ_row[...], jnp.full((1, 128 - NOCC), 99, I32)], axis=1)
    h_lane = jnp.broadcast_to(h_row, (128, 128))
    h_sub = h_lane.T
    same = h_lane == h_sub
    rank_sub = jnp.sum(
        jnp.where(same & (lane < sub), 1.0, 0.0), axis=1, keepdims=True
    ).astype(I32)
    rank_lane = jnp.sum(
        jnp.where(same & (sub < lane), 1.0, 0.0), axis=0, keepdims=True
    ).astype(I32)
    top = jnp.max(jnp.where(sub < NOCC, jnp.broadcast_to(rank_sub, (128, 128)), 0))
    rounds_out[0] = (top >> 5) + 1
    rk = jnp.broadcast_to(rank_sub, (128, 128)) - first_rank
    fits = (rk >= 0) & (rk < SLOT) & (sub < NOCC)
    code = jnp.where(fits, ((rk >> 4) << 7) + (rk & 15), -4096)
    enc[pl.ds(0, 96), :] = jnp.full((96, 128), -1, I32)
    enc[pl.ds(896, 96), :] = jnp.full((96, 128), -1, I32)
    il = (lane >> 4)
    hl = jnp.zeros((128, 128), I32)
    for i in range(PI):
        hi = occ[i]
        hl = jnp.where(il == i, hi, hl)
        value = jnp.where(fits, ((h_sub ^ hi) << 10) + code + 16 * i, -1)
        enc[pl.ds(96 + 100 * i, 100), :] = value[0:100, :]

    g_own = virt[c]
    g_zero = virt[0]

    def class_of(q):
        return virt[4 * r + q] ^ g_own

    s_pad = pad_rows(
        jnp.concatenate([singles[...], jnp.zeros((VB, 128 - NOCC), BF)], axis=1)
    )
    s_own[...] = s_pad

    for q in range(4):
        kq = class_of(q)
        pair_ok = (h_sub ^ hl) == kq
        parts = [
            jnp.where(pair_ok & (code + (il << 4) == lane + 128 * half), 1.0, 0.0).astype(BF)
            for half in range(2)
        ]
        sj[q] = jnp.dot(
            s_pad, jnp.concatenate(parts, axis=1), preferred_element_type=F32
        )

    esub = iota((SLOT, 128), 0)
    elane = iota((SLOT, 128), 1)
    keep = (
        ((h_lane[0:SLOT, :] ^ occ[r]) == (g_zero ^ g_own))
        & (jnp.broadcast_to(rank_lane, (SLOT, 128)) - first_rank == esub)
        & (elane < NOCC)
    )
    expand[...] = jnp.where(keep, 1.0, 0.0).astype(BF)

    def build(step, carry):
        q = step // 2
        start = pl.multiple_of(lax.rem(step, 2) * 496, 16)
        kq = virt[4 * r + q] ^ g_own
        e = enc[pl.ds(start, 496), :]
        l2 = iota((496, 128), 1) + (kq << 10)
        o0 = jnp.where(e == l2, 1.0, 0.0).astype(BF)
        o1 = jnp.where(e == l2 + 128, 1.0, 0.0).astype(BF)
        onehot[q, pl.ds(start, 496), 0:128] = o0
        onehot[q, pl.ds(start, 496), 128:256] = o1
        return carry

    lax.fori_loop(0, 8, build, 0)

    vrow = iota((8, WIN), 0)
    shift = ((vrow & 1) << 6) + (((vrow >> 1) & 1) << 5)
    b_lane = iota((8, WIN), 1) - shift
    inside = (b_lane >= 0) & (b_lane < NV)
    blk = (jnp.where(inside, b_lane, 0) * 5243) >> 17
    g_lane = jnp.full((8, WIN), 99, I32)
    for k in range(NB):
        g_lane = jnp.where(blk == k, virt[k], g_lane)
    g_lane = jnp.where(inside, g_lane, 99)
    for v in range(4):
        for q in range(4):
            want = g_zero ^ class_of(q)
            row = jnp.broadcast_to(g_lane[v : v + 1, :], (32, WIN))
            masks[v, q] = jnp.where(row == want, 1.0, 0.0).astype(BF)

    pl.semaphore_wait(barrier, COLS - 1 + ROWS - 1 + 4 * far.astype(I32))
    my_q = lax.rem(c, 4)

    def singles_copy(t):
        return pltpu.make_async_remote_copy(
            src_ref=s_own,
            dst_ref=s_in.at[my_q],
            send_sem=ssend.at[t],
            recv_sem=srecv.at[my_q],
            device_id=(mate_row, 4 * r + t),
            device_id_type=MESH,
        )

    def singles_wait(t):
        return pltpu.make_async_remote_copy(
            src_ref=s_own,
            dst_ref=s_in.at[t],
            send_sem=ssend.at[t],
            recv_sem=srecv.at[t],
            device_id=(mate_row, 4 * r + t),
            device_id_type=MESH,
        )

    for t in range(4):
        other = far | (my_q != t)

        @pl.when(other)
        def _():
            singles_copy(t).start()

        @pl.when(jnp.logical_not(other))
        def _():
            s_in[t] = s_own[...]

    fsub = iota((128, 256), 0)
    pick = jnp.where(fsub == ((iota((128, 256), 1) & 127) >> 4), 1.0, 0.0).astype(BF)
    for t in range(4):
        other = far | (my_q != t)

        @pl.when(other)
        def _():
            singles_wait(t).wait_send()
            singles_wait(t).wait_recv()

        sc[t] = jnp.dot(s_in[t], pick, preferred_element_type=F32)

    for p in range(2):
        cs[p, 1600:KP, :] = jnp.zeros((KP - 1600, 256), BF)

    def compact(q, carry):
        amp_copy(q).wait()
        for u0 in range(4):
            count = 7 if u0 == 0 else 6
            res4 = lax.rem(q + u0, 4)
            step = (q + u0) // 4
            pieces = []
            for w in range(count):
                base = pl.multiple_of(128 * (25 * w + 6 * u0 + step), 128)
                pieces.append(pad_rows(av[q, :, pl.ds(base, WIN)]))
            left = jnp.concatenate(pieces, axis=0)
            start = pl.multiple_of(96 - 32 * res4, 32)
            got = jnp.dot(
                left, onehot[q, pl.ds(start, WIN), :], preferred_element_type=F32
            )
            par = lax.rem(q + u0, 2)
            half = (25 * q + u0) // 2
            for w in range(count):
                u = u0 + 4 * w
                value = got[32 * w : 32 * w + 32, :] + sc[q, u : u + 1, :] * sj[q]
                at = pl.multiple_of(32 * (half + 2 * w), 32)
                cs[par, pl.ds(at, 32), :] = value.astype(BF)
        return carry

    lax.fori_loop(0, 4, compact, 0)

    def turn(step, carry):
        p = step // 7
        at = pl.multiple_of(lax.rem(step, 7) * 256, 256)
        ct[p, :, pl.ds(at, 256)] = cs[p, pl.ds(at, 256), :].T
        return carry

    lax.fori_loop(0, 14, turn, 0)

    def main_tile(a, lane0, width):
        for p in range(2):
            m = [masks[2 * a + p, q, 0:VB, pl.ds(lane0, width)] > 0 for q in range(4)]
            pieces = []
            for w in range(50):
                k = 2 * w + p
                x = bv[a, :, pl.ds(k * WIN + lane0, width)]
                pieces.append(pad_rows(jnp.where(m[k // 25], x, jnp.zeros_like(x))))
            pieces.append(jnp.zeros((KP - 1600, width), BF))
            right = jnp.concatenate(pieces, axis=0)
            acc[a, p, :, pl.ds(lane0, width)] = jnp.dot(
                ct[p], right, preferred_element_type=F32
            )

    def main_range(a, lo, hi):
        def one(n, carry):
            main_tile(a, pl.multiple_of(n * 256, 256), 256)
            return carry
        lax.fori_loop(lo, hi, one, 0)

    def core_copy(a):
        return pltpu.make_async_remote_copy(
            src_ref=core_out.at[a], dst_ref=core_in.at[a],
            send_sem=csend.at[a], recv_sem=crecv.at[a],
            device_id=(r, partner), device_id_type=MESH,
        )

    def row_copy(a, k):
        to = lax.rem(r + k, ROWS)
        return pltpu.make_async_remote_copy(
            src_ref=qb.at[a, pl.ds(pl.multiple_of(16 * to, 16), 16), :],
            dst_ref=row_in.at[a, k - 1],
            send_sem=rsend.at[a, k - 1], recv_sem=rrecv.at[a, k - 1],
            device_id=(to, c), device_id_type=MESH,
        )

    def wait_int(a):
        pltpu.make_async_copy(bv.at[a], bv.at[a], bsem.at[a]).wait()

    def join(a):
        odd = acc[a, 1]
        odd = jnp.concatenate([odd[:, 64:], jnp.zeros((256, 64), F32)], axis=1)
        acc[a, 0] = acc[a, 0] + odd
        give = pl.multiple_of((1 - core) * 128, 128)
        core_out[a] = acc[a, 0, pl.ds(give, 128), :].astype(BF)
        core_copy(a).start()

    def spread(a):
        core_copy(a).wait()
        keep_at = pl.multiple_of(core * 128, 128)
        total = acc[a, 0, pl.ds(keep_at, 128), :] + core_in[a].astype(F32)
        qf[a] = total
        qb[a] = total.astype(BF)
        for k in range(1, ROWS):
            row_copy(a, k).start()

    wait_int(0)
    main_range(0, 0, 3)
    main_tile(0, 768, 128)
    join(0)
    wait_int(1)
    main_range(1, 0, 2)
    spread(0)
    main_range(1, 2, 3)
    main_tile(1, 768, 128)
    join(1)
    spread(1)

    for a in range(2):
        total = qf[a, pl.ds(pl.multiple_of(16 * r, 16), 16), :]
        for k in range(1, ROWS):
            row_copy(a, k).wait()
            total = total + row_in[a, k - 1].astype(F32)
        wsum[a] = total

    zlane = iota((16, 128), 1)
    for t in range(16):
        sides = []
        for a in range(2):
            begin = 32 * a + 50 * t
            tile, s = begin // 128, begin % 128
            to = 64 * a
            turn_by = (to - s) % 128
            x = wsum[a, :, tile * 128 : tile * 128 + 128]
            if turn_by:
                x = pltpu.roll(x, turn_by, 1)
            if s + 50 > 128:
                y = wsum[a, :, tile * 128 + 128 : tile * 128 + 256]
                if turn_by:
                    y = pltpu.roll(y, turn_by, 1)
                x = jnp.where(zlane - to + s < 128, x, y)
            sides.append(x)
        z = jnp.where(zlane < 64, sides[0], sides[1])
        zf[t] = z
        zb[t] = z.astype(BF)

    def col_copy(k):
        to = lax.rem(c + k, COLS)
        return pltpu.make_async_remote_copy(
            src_ref=zb.at[to // 2], dst_ref=col_in.at[k - 1],
            send_sem=zsend.at[k - 1], recv_sem=zrecv.at[k - 1],
            device_id=(r, to), device_id_type=MESH,
        )

    def start_col(k, carry):
        col_copy(k).start()
        return carry

    lax.fori_loop(1, COLS, start_col, 0)
    mine = zf[c // 2]
    other = jnp.zeros((16, 128), F32)
    for k in range(1, COLS):
        col_copy(k).wait()
        part = col_in[k - 1].astype(F32)
        if k % 2:
            other = other + part
        else:
            mine = mine + part
    res[pl.ds(pl.multiple_of(core * 16, 16), 16), :] = mine
    res[pl.ds(pl.multiple_of((1 - core) * 16, 16), 16), :] = other

    osub = iota((64, 128), 0)
    b_own = osub & 31
    wanted = ((osub >> 5) << 6) + core * VB + b_own
    select = jnp.where((iota((64, 128), 1) == wanted) & (b_own < VB), 1.0, 0.0).astype(BF)
    narrow = lax.dot_general(
        select, res[...].astype(BF), (((1,), (1,)), ((), ())), preferred_element_type=F32
    ).astype(BF)
    final = jnp.dot(narrow, expand[...], preferred_element_type=F32).astype(BF)
    for a in range(2):
        out[a] = final[32 * a : 32 * a + VB, 0:NOCC]


def run_round(index, amplitudes, singles_t, integrals, virt_irrep, occ_irrep):
    smem = pl.BlockSpec(memory_space=pltpu.SMEM)
    vmem = pl.BlockSpec(memory_space=pltpu.VMEM)
    hbm = pl.BlockSpec(memory_space=pl.ANY)
    dma = pltpu.SemaphoreType.DMA
    return pl.pallas_call(
        kernel,
        out_shape=(
            jax.ShapeDtypeStruct((2, VB, NOCC), BF),
            jax.ShapeDtypeStruct((1,), I32),
        ),
        in_specs=[smem, smem, smem, vmem, vmem, hbm, hbm],
        out_specs=(vmem, smem),
        scratch_shapes=[
            pltpu.VMEM((4, VB, ALEN), BF),
            pltpu.VMEM((2, VB, NC * WIN), BF),
            pltpu.VMEM((992, 128), I32),
            pltpu.VMEM((4, 992, 256), BF),
            pltpu.VMEM((2, KP, 256), BF),
            pltpu.VMEM((2, 256, KP), BF),
            pltpu.VMEM((4, 4, 32, WIN), BF),
            pltpu.VMEM((2, 2, 256, WIN), F32),
            pltpu.VMEM((4, 32, 256), F32),
            pltpu.VMEM((4, 32, 256), F32),
            pltpu.VMEM((32, 128), BF),
            pltpu.VMEM((4, 32, 128), BF),
            pltpu.VMEM((SLOT, 128), BF),
            pltpu.VMEM((2, 128, WIN), BF),
            pltpu.VMEM((2, 128, WIN), BF),
            pltpu.VMEM((2, 128, WIN), F32),
            pltpu.VMEM((2, 128, WIN), BF),
            pltpu.VMEM((2, ROWS - 1, 16, WIN), BF),
            pltpu.VMEM((2, 16, WIN), F32),
            pltpu.VMEM((16, 16, 128), BF),
            pltpu.VMEM((16, 16, 128), F32),
            pltpu.VMEM((COLS - 1, 16, 128), BF),
            pltpu.VMEM((SLOT, 128), F32),
            dma((4,)), dma((2,)), dma((4,)), dma((4,)), dma((2,)), dma((2,)),
            dma((2, ROWS - 1)), dma((2, ROWS - 1)), dma((COLS - 1,)), dma((COLS - 1,)),
        ],
        compiler_params=pltpu.CompilerParams(
            collective_id=0, has_side_effects=True, vmem_limit_bytes=50 * 1024 * 1024
        ),
        name="ladder_round",
    )(
        index, virt_irrep, occ_irrep, occ_irrep.reshape(1, NOCC), singles_t,
        amplitudes, integrals,
    )


def body(amplitudes, singles, integrals, virt_irrep, occ_irrep):
    singles_t = jnp.transpose(singles)

    def more(state):
        return state[0] < state[1][0]

    def step(state):
        index, _, total = state
        part, rounds = run_round(
            jnp.full((1,), index, I32), amplitudes, singles_t, integrals, virt_irrep, occ_irrep
        )
        return index + 1, rounds, total + part

    start = (jnp.int32(0), jnp.ones((1,), I32), jnp.zeros((2, VB, NOCC), BF))
    _, _, total = lax.while_loop(more, step, start)
    return jnp.transpose(total, (2, 0, 1))


def solution(mesh):
    placed = (P("col", "row"), P(None, "col"), P("col", "row"), P(), P())
    return jax.shard_map(
        body, mesh=mesh, in_specs=placed, out_specs=P("row", None, "col"), check_vma=False
    )
```

```python
import functools

import jax
import jax.numpy as jnp
from jax import lax
from jax.experimental import pallas as pl
from jax.experimental.pallas import tpu as pltpu
from jax.sharding import PartitionSpec as P

MESH = pl.DeviceIdType.MESH
BF = jnp.bfloat16
F32 = jnp.float32
I32 = jnp.int32

VB = 25
NB = 32
NOCC = 100
PI = 8
ROWS, COLS = 8, 32
NC = 100
SLOT = 24
PR = PI * SLOT
WIN = 896
ALEN = 157 * 128
KP = 3328
KH = KP // 2
BCH = 5
BLEN = 20 * 1600
NW = 13 * 128
NV = 800


def iota(shape, dim):
    return lax.broadcasted_iota(I32, shape, dim)


def pad_rows(x):
    return jnp.concatenate([x, jnp.zeros((32 - x.shape[0], x.shape[1]), x.dtype)], axis=0)


def one(cond):
    return jnp.where(cond, 1.0, 0.0).astype(BF)


def kernel(
    round_ref, virt, occ, occ_row, singles, amp, integ,
    out, rounds_out,
    av, bv, enc, onehot, cs, rt, ct, masks, bm, sjx, spread_c, acc, psum, s_own, s_in, expand,
    core_out, core_in, qf, qb, xy_in, zf, zb, z_in,
    asem, bsem, ssend, srecv, csend, crecv, rsend, rrecv, zsend, zrecv,
):
    r = lax.axis_index("row")
    c = lax.axis_index("col")
    x = lax.rem(r, 4)
    y_lo = r // 4
    z = c // 4
    y_hi = lax.rem(c // 2, 2)
    core = lax.rem(c, 2)
    y = 2 * y_hi + y_lo

    def device(x, y, z, core):
        return lax.rem(y, 2) * 4 + x, z * 4 + (y // 2) * 2 + core

    def copy_to(where, src, dst, send, recv):
        return pltpu.make_async_remote_copy(
            src_ref=src, dst_ref=dst, send_sem=send, recv_sem=recv,
            device_id=where, device_id_type=MESH,
        )

    def amp_copy(q):
        return pltpu.make_async_copy(
            amp.at[:, pl.ds(pl.multiple_of(q * (156 * 128), 128), ALEN)], av.at[q], asem.at[q]
        )

    def int_copy(k):
        return pltpu.make_async_copy(
            integ.at[:, pl.ds(pl.multiple_of(k * BLEN, 128), BLEN)], bv.at[k], bsem.at[k]
        )

    for q in range(4):
        amp_copy(q).start()
    for k in range(BCH):
        int_copy(k).start()

    barrier = pltpu.get_barrier_semaphore()
    at_home = r == z
    is_source = x == lax.rem(z, 4)
    target_y = jnp.where(y_lo == z // 4, y, 3 - y)

    def greet(where):
        pl.semaphore_signal(barrier, inc=1, device_id=where, device_id_type=MESH)

    for sy in (y, 3 - y):
        for sc in range(2):
            me = at_home & (sc == core) if sy is y else False
            if sy is y:
                @pl.when(jnp.logical_not(me))
                def _():
                    greet(device(x, sy, r, sc))
            else:
                greet(device(x, sy, r, sc))

    def z_peer(k):
        return device(x, y, lax.rem(z + k, 8), core)

    def z_cross(k):
        return device(x, y, lax.rem(z + k, 8), 1 - core)

    def xy_peer(k):
        return device(lax.rem(x + lax.rem(k, 4), 4), lax.rem(y + k // 4, 4), z, core)

    partner = device(x, y, z, 1 - core)

    def greet_z(k, carry):
        greet(z_peer(k))
        greet(z_cross(k))
        return carry

    def greet_xy(k, carry):
        greet(xy_peer(k))
        return carry

    lax.fori_loop(1, 8, greet_z, 0)
    lax.fori_loop(1, 16, greet_xy, 0)
    greet(partner)

    first_rank = round_ref[0] * SLOT
    lane = iota((128, 128), 1)
    sub = iota((128, 128), 0)
    h_row = jnp.concatenate([occ_row[...], jnp.full((1, 128 - NOCC), 99, I32)], axis=1)
    h_lane = jnp.broadcast_to(h_row, (128, 128))
    h_sub = h_lane.T
    same = h_lane == h_sub
    rank_sub = jnp.broadcast_to(
        jnp.sum(jnp.where(same & (lane < sub), 1.0, 0.0), axis=1, keepdims=True).astype(I32),
        (128, 128),
    )
    rank_lane = jnp.sum(
        jnp.where(same & (sub < lane), 1.0, 0.0), axis=0, keepdims=True
    ).astype(I32)
    top = jnp.max(jnp.where(sub < NOCC, rank_sub, 0))
    rounds_out[0] = sum((top >= SLOT * k).astype(I32) for k in range(5))
    rk = rank_sub - first_rank
    fits = (rk >= 0) & (rk < SLOT) & (sub < NOCC)
    enc[pl.ds(0, 96), :] = jnp.full((96, 128), -1, I32)
    enc[pl.ds(896, 96), :] = jnp.full((96, 128), -1, I32)
    for i in range(PI):
        code = jnp.where(rk < 16, rk + 16 * i, rk + (112 + 8 * i))
        value = jnp.where(fits, ((h_sub ^ occ[i]) << 10) + code, -1)
        enc[pl.ds(96 + 100 * i, 100), :] = value[0:100, :]

    g_own = virt[c]
    g_zero = virt[0]

    def build(step, carry):
        q = step // 2
        start = pl.multiple_of(lax.rem(step, 2) * 496, 16)
        kq = virt[4 * r + q] ^ g_own
        e = enc[pl.ds(start, 496), :]
        l2 = iota((496, 128), 1) + (kq << 10)
        onehot[q, pl.ds(start, 496), 0:128] = one(e == l2)
        onehot[q, pl.ds(start, 496), 128:256] = one(e == l2 + 128)
        return carry

    lax.fori_loop(0, 8, build, 0)

    my_q = lax.rem(c, 4)
    s_pad = pad_rows(
        jnp.concatenate([singles[...], jnp.zeros((VB, 128 - NOCC), BF)], axis=1)
    )
    place = one(iota((32, 128), 1) == iota((32, 128), 0) + VB * my_q)
    place = jnp.where(iota((32, 128), 0) < VB, place.astype(F32), 0.0).astype(BF)
    s_own[...] = lax.dot_general(
        s_pad[:, 0:16], place, (((0,), (0,)), ((), ())), preferred_element_type=F32
    ).astype(BF)

    for p in range(2):
        cs[KH * p + 1600 : KH * p + KH, :] = jnp.zeros((KH - 1600, 256), BF)

    def compact(q, carry):
        amp_copy(q).wait()
        for u0 in range(4):
            count = 7 if u0 == 0 else 6
            step = (q + u0) // 4
            pieces = []
            for w in range(count):
                base = pl.multiple_of(128 * (25 * w + 6 * u0 + step), 128)
                pieces.append(pad_rows(av[q, :, pl.ds(base, WIN)]))
            left = jnp.concatenate(pieces, axis=0)
            start = pl.multiple_of(96 - 32 * lax.rem(q + u0, 4), 32)
            got = jnp.dot(
                left, onehot[q, pl.ds(start, WIN), :], preferred_element_type=F32
            ).astype(BF)
            at0 = KH * lax.rem(q + u0, 2) + 32 * ((25 * q + u0) // 2)
            for w in range(count):
                at = pl.multiple_of(at0 + 64 * w, 32)
                cs[pl.ds(at, 32), :] = got[32 * w : 32 * w + 32, :]
        return carry

    lax.fori_loop(0, 4, compact, 0)

    def turn(step, carry):
        at = pl.multiple_of(step * 256, 256)
        rt[:, pl.ds(at, 256)] = cs[pl.ds(at, 256), :].T[0:PR, :]
        return carry

    lax.fori_loop(0, KP // 256, turn, 0)

    pl.semaphore_wait(
        barrier,
        30 + jnp.where(is_source, 16, 0) - jnp.where(is_source & at_home, 1, 0),
    )

    def singles_copy(k):
        tz, tc = k // 2, lax.rem(k, 2)
        return copy_to(
            device(x, target_y, tz, tc), s_own, s_in.at[my_q], ssend.at[k], srecv.at[my_q]
        )

    def not_me(k):
        return jnp.logical_not(at_home & (k // 2 == z) & (lax.rem(k, 2) == core))

    @pl.when(is_source)
    def _():
        def send(k, carry):
            @pl.when(not_me(k))
            def _():
                singles_copy(k).start()
            return carry
        lax.fori_loop(0, 16, send, 0)

    for p in range(2):
        col_at = iota((8, NW), 1) - 64 * p
        b_at = jnp.where(col_at >= NV, col_at - NV, jnp.where(col_at < 0, 0, col_at))
        b_block = (b_at * 5243) >> 17
        g_lane = jnp.full((8, NW), 99, I32)
        for k in range(NB):
            g_lane = jnp.where(b_block == k, virt[k], g_lane)
        g_lane = jnp.where((col_at >= 0) & (col_at < 2 * NV), g_lane, 99)
        for q in range(4):
            want = g_zero ^ g_own ^ virt[4 * r + q]
            masks[p, q] = one(jnp.broadcast_to(g_lane[0:1, :], (32, NW)) == want)

    for p in range(2):
        bm[p, 1600:KH, :] = jnp.zeros((KH - 1600, NW), BF)

    def arrange(k, carry):
        @pl.when(lax.rem(k, 10) == 0)
        def _():
            int_copy(k // 10).wait()
        ch, w = k // 10, lax.rem(k, 10)
        row = pl.multiple_of(32 * k, 32)
        for p in range(2):
            q = (2 * k + p) // 25
            for n in range(13):
                v = bv[ch, :, pl.ds(pl.multiple_of(128 * (25 * w + 12 * p + n), 128), 128)]
                ok = masks[p, q, 0:VB, n * 128 : n * 128 + 128] > 0
                v = jnp.where(ok, v, jnp.zeros_like(v))
                bm[p, pl.ds(row, 32), n * 128 : n * 128 + 128] = pad_rows(v)
        return carry

    lax.fori_loop(0, NC // 2, arrange, 0)

    prow = iota((PR, 128), 0)
    late = prow >= 128
    slot = jnp.where(late, 16 + (prow & 7), prow & 15)
    i_row = jnp.where(late, (prow - 128) >> 3, prow >> 4)
    h_i = jnp.zeros((PR, 128), I32)
    for i in range(PI):
        h_i = jnp.where(i_row == i, occ[i], h_i)
    slot_ok = (jnp.broadcast_to(rank_lane, (PR, 128)) - first_rank) == slot
    pair_class = jnp.broadcast_to(h_row, (PR, 128)) ^ h_i
    s_t = lax.dot_general(
        s_pad, one(iota((32, 128), 0) == (iota((32, 128), 1) & 31)),
        (((0,), (0,)), ((), ())), preferred_element_type=F32,
    ).astype(BF)
    by_class = [
        jnp.dot(
            one(slot_ok & (pair_class == (virt[4 * r + q] ^ g_own))), s_t,
            preferred_element_type=F32,
        )
        for q in range(4)
    ]
    plane = iota((PR, 128), 1)
    for tile in range(KP // 128):
        begin = 8 * (tile % 13) + tile // 13
        low, high = min(3, begin // VB), min(3, (begin + 6) // VB)
        value = by_class[low]
        if low != high:
            value = jnp.where(2 * (plane >> 5) + begin < VB * high, value, by_class[high])
        sjx[:, tile * 128 : tile * 128 + 128] = value
    for p in range(2):
        c_at = 2 * (iota((128, KH), 1) >> 5) + p
        spread_c[:, KH * p : KH * p + KH] = one(iota((128, KH), 0) == c_at)

    erow = iota((32, 128), 0)
    keep = (
        ((h_lane[0:32, :] ^ occ[r]) == (g_zero ^ g_own))
        & (jnp.broadcast_to(rank_lane, (32, 128)) - first_rank == erow)
        & (iota((32, 128), 1) < NOCC)
        & (erow < SLOT)
    )
    expand[...] = one(keep)

    @pl.when(is_source)
    def _():
        def sent(k, carry):
            @pl.when(not_me(k))
            def _():
                singles_copy(k).wait_send()
            return carry
        lax.fori_loop(0, 16, sent, 0)

    for t in range(4):
        me = at_home & (my_q == t)

        @pl.when(jnp.logical_not(me))
        def _():
            copy_to(partner, s_own, s_in.at[t], ssend.at[t], srecv.at[t]).wait_recv()

        @pl.when(me)
        def _():
            s_in[t] = s_own[...]

    pack = s_in[0].astype(F32)
    for t in range(1, 4):
        pack = pack + s_in[t].astype(F32)
    first = jnp.dot(pack.astype(BF), spread_c[...], preferred_element_type=F32)
    for tile in range(KP // 128):
        cols = slice(tile * 128, tile * 128 + 128)
        for block in range(PR // 16):
            rows = slice(16 * block, 16 * block + 16)
            if block < PI:
                left = jnp.broadcast_to(first[block : block + 1, cols], (16, 128))
            else:
                i = 2 * (block - PI)
                left = jnp.concatenate(
                    [jnp.broadcast_to(first[k : k + 1, cols], (8, 128)) for k in (i, i + 1)],
                    axis=0,
                )
            value = rt[rows, cols].astype(F32) + left * sjx[rows, cols]
            ct[rows, cols] = value.astype(BF)

    def main(lo, hi):
        for p in range(2):
            acc[p, :, lo:hi] = jnp.dot(
                ct[:, KH * p : KH * p + KH], bm[p, :, lo:hi], preferred_element_type=F32
            )

    core_copy = copy_to(partner, core_out, core_in, csend, crecv)

    def xy_copy(k):
        row, col = xy_peer(k)
        src = qb.at[
            pl.ds(pl.multiple_of(16 * row, 16), 16),
            pl.ds(pl.multiple_of(lax.rem(col // 2, 2) * 768, 128), 768),
        ]
        return copy_to((row, col), src, xy_in.at[k - 1], rsend.at[k - 1], rrecv.at[k - 1])

    wide = iota((PR, 128), 1)

    def start_of(a):
        return 0 if a == 0 else 768

    def summed_tile(a, n):
        n = n + start_of(a) // 128
        cols = slice(n * 128, n * 128 + 128)
        value = acc[0, :, cols]
        turned = pltpu.roll(acc[1, :, cols], 64, 1)
        after = 0.0
        if n < NW // 128 - 1:
            after = pltpu.roll(acc[1, :, n * 128 + 128 : n * 128 + 256], 64, 1)
        return value + jnp.where(wide < 64, turned, after)

    def give(a):
        for n in range(7):
            core_out[:, n * 128 : n * 128 + 128] = summed_tile(a, n).astype(BF)
        core_copy.start()

    def keep_own(a):
        for n in range(7):
            psum[:, n * 128 : n * 128 + 128] = summed_tile(a, n)

    def spread(a):
        core_copy.wait_recv()
        total = psum[...] + core_in[...].astype(F32)
        for yh in range(2):
            tiles = []
            for pair in range(4):
                sides = []
                for odd in range(2):
                    begin = NV * a - start_of(a) + 200 * pair + 100 * odd + 50 * yh
                    tile, s = begin // 128, begin % 128
                    by = (64 * odd - s) % 128
                    v = total[:, tile * 128 : tile * 128 + 128]
                    v = pltpu.roll(v, by, 1) if by else v
                    if s + 50 > 128:
                        u = total[:, tile * 128 + 128 : tile * 128 + 256]
                        u = pltpu.roll(u, by, 1) if by else u
                        v = jnp.where(wide < 64 * odd + 128 - s, v, u)
                    sides.append(v)
                v = jnp.where(wide < 64, sides[0], sides[1])
                tiles.append(v)
                cols = slice(yh * 768 + pair * 128, yh * 768 + pair * 128 + 128)
                qf[:, cols] = v[0:128, :]
                qb[:, cols] = v[0:128, :].astype(BF)
            for e in range(2):
                cols = slice(yh * 768 + 512 + e * 128, yh * 768 + 640 + e * 128)
                for i in range(PI):
                    v = jnp.concatenate(
                        [tiles[e + 2 * k][128 + 8 * i : 136 + 8 * i, :] for k in range(2)], axis=0
                    )
                    qf[16 * i : 16 * i + 16, cols] = v
                    qb[16 * i : 16 * i + 16, cols] = v.astype(BF)

        def start_xy(k, carry):
            xy_copy(k).start()
            return carry
        lax.fori_loop(1, 16, start_xy, 0)

    main(0, 1024)

    @pl.when(core == 1)
    def _():
        give(0)

    @pl.when(core == 0)
    def _():
        keep_own(0)

    main(1024, NW)

    @pl.when(core == 0)
    def _():
        give(1)
        spread(0)

    @pl.when(core == 1)
    def _():
        keep_own(1)
        spread(1)

    total = qf[
        pl.ds(pl.multiple_of(16 * r, 16), 16),
        pl.ds(pl.multiple_of(768 * y_hi, 128), 768),
    ]
    for k in range(1, 16):
        xy_copy(k).wait_recv()
        total = total + xy_in[k - 1].astype(F32)

    def z_copy(to, to_core):
        return copy_to(
            device(x, y, to, to_core), zb.at[to], z_in.at[core, z],
            zsend.at[to_core, to], zrecv.at[core, z],
        )

    zlane = iota((16, 128), 1)
    zsub = iota((16, 128), 0)
    for to in range(8):
        pair, odd = to // 2, to % 2
        early = total[:, pair * 128 : pair * 128 + 128]
        late8 = total[:, 512 + (pair % 2) * 128 : 640 + (pair % 2) * 128]
        if pair // 2:
            late8 = jnp.concatenate([late8[8:16, :], late8[0:8, :]], axis=0)
        if odd:
            early = pltpu.roll(early, 64, 1)
        else:
            late8 = pltpu.roll(late8, 64, 1)
        part = jnp.where(zlane < 64, early, jnp.where(zsub < 8, late8, 0.0))
        zf[to] = part
        zb[to] = part.astype(BF)
        for to_core in range(2):
            @pl.when(jnp.logical_not((z == to) & (core == to_core)))
            def _():
                z_copy(to, to_core).start()

    core_copy.wait_send()
    for k in range(1, 16):
        xy_copy(k).wait_send()
    z_in[core, z] = jnp.zeros((16, 128), BF)
    sums = []
    for a in range(2):
        value = jnp.where(core == a, zf[z], 0.0)
        for k in range(8):
            @pl.when(jnp.logical_not((z == k) & (core == a)))
            def _():
                copy_to(partner, zb.at[k], z_in.at[a, k], zsend.at[a, k], zrecv.at[a, k]).wait()
            value = value + z_in[a, k].astype(F32)
        sums.append(value.astype(BF))

    osub = iota((64, 128), 0)
    b_own = osub & 31
    wanted = ((osub >> 5) << 6) + core * VB + b_own
    select = one((iota((64, 128), 1) == wanted) & (b_own < VB))
    for a in range(2):
        narrow = lax.dot_general(
            select, sums[a], (((1,), (1,)), ((), ())), preferred_element_type=F32
        ).astype(BF)
        final = jnp.dot(narrow[0:32, :], expand[0:16, :], preferred_element_type=F32)
        final = final + jnp.dot(narrow[32:64, :], expand[16:32, :], preferred_element_type=F32)
        out[a] = final.astype(BF)[0:VB, 0:NOCC]


def run_round(index, amplitudes, singles_t, integrals, virt_irrep, occ_irrep):
    smem = pl.BlockSpec(memory_space=pltpu.SMEM)
    vmem = pl.BlockSpec(memory_space=pltpu.VMEM)
    hbm = pl.BlockSpec(memory_space=pl.ANY)
    dma = pltpu.SemaphoreType.DMA
    return pl.pallas_call(
        kernel,
        out_shape=(
            jax.ShapeDtypeStruct((2, VB, NOCC), BF),
            jax.ShapeDtypeStruct((1,), I32),
        ),
        in_specs=[smem, smem, smem, vmem, vmem, hbm, hbm],
        out_specs=(vmem, smem),
        scratch_shapes=[
            pltpu.VMEM((4, VB, ALEN), BF),
            pltpu.VMEM((BCH, VB, BLEN), BF),
            pltpu.VMEM((992, 128), I32),
            pltpu.VMEM((4, 992, 256), BF),
            pltpu.VMEM((KP, 256), BF),
            pltpu.VMEM((PR, KP), BF),
            pltpu.VMEM((PR, KP), BF),
            pltpu.VMEM((2, 4, 32, NW), BF),
            pltpu.VMEM((2, KH, NW), BF),
            pltpu.VMEM((PR, KP), F32),
            pltpu.VMEM((128, KP), BF),
            pltpu.VMEM((2, PR, NW), F32),
            pltpu.VMEM((PR, 896), F32),
            pltpu.VMEM((16, 128), BF),
            pltpu.VMEM((4, 16, 128), BF),
            pltpu.VMEM((32, 128), BF),
            pltpu.VMEM((PR, 896), BF),
            pltpu.VMEM((PR, 896), BF),
            pltpu.VMEM((128, 1536), F32),
            pltpu.VMEM((128, 1536), BF),
            pltpu.VMEM((15, 16, 768), BF),
            pltpu.VMEM((8, 16, 128), F32),
            pltpu.VMEM((8, 16, 128), BF),
            pltpu.VMEM((2, 8, 16, 128), BF),
            dma((4,)), dma((BCH,)), dma((16,)), dma((4,)), dma, dma,
            dma((15,)), dma((15,)), dma((2, 8)), dma((2, 8)),
        ],
        compiler_params=pltpu.CompilerParams(
            collective_id=0, has_side_effects=True, vmem_limit_bytes=58 * 1024 * 1024
        ),
        name="ladder_round",
    )(
        index, virt_irrep, occ_irrep, occ_irrep.reshape(1, NOCC), singles_t,
        amplitudes, integrals,
    )


def body(amplitudes, singles, integrals, virt_irrep, occ_irrep):
    singles_t = jnp.transpose(singles)

    def more(state):
        return state[0] < state[1][0]

    def step(state):
        index, _, total = state
        part, rounds = run_round(
            jnp.full((1,), index, I32), amplitudes, singles_t, integrals, virt_irrep, occ_irrep
        )
        return index + 1, rounds, total + part

    start = (jnp.int32(0), jnp.ones((1,), I32), jnp.zeros((2, VB, NOCC), BF))
    _, _, total = lax.while_loop(more, step, start)
    return jnp.transpose(total, (2, 0, 1))


def solution(mesh):
    placed = (P("col", "row"), P(None, "col"), P("col", "row"), P(), P())
    return jax.shard_map(
        body, mesh=mesh, in_specs=placed, out_specs=P("row", None, "col"), check_vma=False
    )
```

```python
import functools

import jax
import jax.numpy as jnp
from jax import lax
from jax.experimental import pallas as pl
from jax.experimental.pallas import tpu as pltpu
from jax.sharding import PartitionSpec as P

MESH = pl.DeviceIdType.MESH
BF = jnp.bfloat16
F32 = jnp.float32
I32 = jnp.int32

VB = 25
NB = 32
NOCC = 100
PI = 8
ROWS, COLS = 8, 32
NC = 100
SLOT = 24
PR = PI * SLOT
WIN = 896
ALEN = 157 * 128
KP = 3328
KH = KP // 2
BCH = 5
BLEN = 20 * 1600
NW = 13 * 128
NV = 800
Z_ORDER = (4, 3, 5, 2, 6, 1, 7)
XY_ORDER = (10, 6, 9, 11, 14, 2, 5, 7, 8, 13, 15, 1, 3, 4, 12)


def iota(shape, dim):
    return lax.broadcasted_iota(I32, shape, dim)


def pad_rows(x):
    return jnp.concatenate([x, jnp.zeros((32 - x.shape[0], x.shape[1]), x.dtype)], axis=0)


def one(cond):
    return jnp.where(cond, 1.0, 0.0).astype(BF)


def kernel(
    round_ref, virt, occ, occ_row, singles, amp, integ,
    out, rounds_out,
    av, bv, enc, onehot, cs, rt, ct, masks, bm, sjx, spread_c, acc, psum, s_own, s_in, expand,
    core_out, core_in, qf, qb, xy_in, zf, zb, z_in,
    asem, bsem, ssend, srecv, csend, crecv, rsend, rrecv, zsend, zrecv,
):
    r = lax.axis_index("row")
    c = lax.axis_index("col")
    x = lax.rem(r, 4)
    y_lo = r // 4
    z = c // 4
    y_hi = lax.rem(c // 2, 2)
    core = lax.rem(c, 2)
    y = 2 * y_hi + y_lo

    def device(x, y, z, core):
        return lax.rem(y, 2) * 4 + x, z * 4 + (y // 2) * 2 + core

    def copy_to(where, src, dst, send, recv):
        return pltpu.make_async_remote_copy(
            src_ref=src, dst_ref=dst, send_sem=send, recv_sem=recv,
            device_id=where, device_id_type=MESH,
        )

    def amp_copy(q):
        return pltpu.make_async_copy(
            amp.at[:, pl.ds(pl.multiple_of(q * (156 * 128), 128), ALEN)], av.at[q], asem.at[q]
        )

    def int_copy(k):
        return pltpu.make_async_copy(
            integ.at[:, pl.ds(pl.multiple_of(k * BLEN, 128), BLEN)], bv.at[k], bsem.at[k]
        )

    for q in range(4):
        amp_copy(q).start()
    for k in range(BCH):
        int_copy(k).start()

    barrier = pltpu.get_barrier_semaphore()
    at_home = r == z
    is_source = x == lax.rem(z, 4)
    target_y = jnp.where(y_lo == z // 4, y, 3 - y)

    def greet(where):
        pl.semaphore_signal(barrier, inc=1, device_id=where, device_id_type=MESH)

    def wrap(v, n):
        return jnp.where(v >= n, v - n, v)

    def z_peer(k, to_core):
        return device(x, y, wrap(z + k, 8), to_core)

    def xy_peer(k):
        return device(wrap(x + k % 4, 4), wrap(y + k // 4, 4), z, core)

    partner = device(x, y, z, 1 - core)

    for sc in range(2):
        greet(device(x, 3 - y, r, sc))
    for sc in range(2):
        @pl.when(jnp.logical_not(at_home & (sc == core)))
        def _():
            greet(device(x, y, r, sc))
    for k in Z_ORDER:
        for sc in range(2):
            greet(z_peer(k, sc))
    for k in XY_ORDER:
        greet(xy_peer(k))
    greet(partner)

    first_rank = round_ref[0] * SLOT
    lane = iota((128, 128), 1)
    sub = iota((128, 128), 0)
    h_row = jnp.concatenate([occ_row[...], jnp.full((1, 128 - NOCC), 99, I32)], axis=1)
    h_lane = jnp.broadcast_to(h_row, (128, 128))
    h_sub = h_lane.T
    same = h_lane == h_sub
    rank_sub = jnp.broadcast_to(
        jnp.sum(jnp.where(same & (lane < sub), 1.0, 0.0), axis=1, keepdims=True).astype(I32),
        (128, 128),
    )
    rank_lane = jnp.sum(
        jnp.where(same & (sub < lane), 1.0, 0.0), axis=0, keepdims=True
    ).astype(I32)
    top = jnp.max(jnp.where(sub < NOCC, rank_sub, 0))
    rounds_out[0] = sum((top >= SLOT * k).astype(I32) for k in range(5))
    rk = rank_sub - first_rank
    fits = (rk >= 0) & (rk < SLOT) & (sub < NOCC)
    enc[pl.ds(0, 96), :] = jnp.full((96, 128), -1, I32)
    enc[pl.ds(896, 96), :] = jnp.full((96, 128), -1, I32)
    for i in range(PI):
        code = jnp.where(rk < 16, rk + 16 * i, rk + (112 + 8 * i))
        value = jnp.where(fits, ((h_sub ^ occ[i]) << 10) + code, -1)
        enc[pl.ds(96 + 100 * i, 100), :] = value[0:100, :]

    g_own = virt[c]
    g_zero = virt[0]

    def build(step, carry):
        q = step // 2
        start = pl.multiple_of(lax.rem(step, 2) * 496, 16)
        kq = virt[4 * r + q] ^ g_own
        e = enc[pl.ds(start, 496), :]
        l2 = iota((496, 128), 1) + (kq << 10)
        onehot[q, pl.ds(start, 496), 0:128] = one(e == l2)
        onehot[q, pl.ds(start, 496), 128:256] = one(e == l2 + 128)
        return carry

    lax.fori_loop(0, 8, build, 0)

    my_q = lax.rem(c, 4)
    s_pad = pad_rows(
        jnp.concatenate([singles[...], jnp.zeros((VB, 128 - NOCC), BF)], axis=1)
    )
    place = one(iota((32, 128), 1) == iota((32, 128), 0) + VB * my_q)
    place = jnp.where(iota((32, 128), 0) < VB, place.astype(F32), 0.0).astype(BF)
    s_own[...] = lax.dot_general(
        s_pad[:, 0:16], place, (((0,), (0,)), ((), ())), preferred_element_type=F32
    ).astype(BF)

    for p in range(2):
        cs[KH * p + 1600 : KH * p + KH, :] = jnp.zeros((KH - 1600, 256), BF)

    def compact(q, carry):
        amp_copy(q).wait()
        for u0 in range(4):
            count = 7 if u0 == 0 else 6
            step = (q + u0) // 4
            pieces = []
            for w in range(count):
                base = pl.multiple_of(128 * (25 * w + 6 * u0 + step), 128)
                pieces.append(pad_rows(av[q, :, pl.ds(base, WIN)]))
            left = jnp.concatenate(pieces, axis=0)
            start = pl.multiple_of(96 - 32 * lax.rem(q + u0, 4), 32)
            got = jnp.dot(
                left, onehot[q, pl.ds(start, WIN), :], preferred_element_type=F32
            ).astype(BF)
            at0 = KH * lax.rem(q + u0, 2) + 32 * ((25 * q + u0) // 2)
            for w in range(count):
                at = pl.multiple_of(at0 + 64 * w, 32)
                cs[pl.ds(at, 32), :] = got[32 * w : 32 * w + 32, :]
        return carry

    lax.fori_loop(0, 4, compact, 0)

    pl.semaphore_wait(
        barrier,
        30 + jnp.where(is_source, 16, 0) - jnp.where(is_source & at_home, 1, 0),
    )

    def singles_copy(k, tc):
        return copy_to(
            device(x, target_y, wrap(z + k, 8), tc), s_own, s_in.at[my_q],
            ssend.at[2 * k + tc], srecv.at[my_q],
        )

    def for_targets(act):
        for k in Z_ORDER:
            for tc in range(2):
                act(singles_copy(k, tc))
        for tc in range(2):
            @pl.when(jnp.logical_not(at_home & (tc == core)))
            def _():
                act(singles_copy(0, tc))

    @pl.when(is_source)
    def _():
        for_targets(lambda copy: copy.start())

    def turn(step, carry):
        at = pl.multiple_of(step * 256, 256)
        rt[:, pl.ds(at, 256)] = cs[pl.ds(at, 256), :].T[0:PR, :]
        return carry

    lax.fori_loop(0, KP // 256, turn, 0)

    for p in range(2):
        col_at = iota((8, NW), 1) - 64 * p
        b_at = jnp.where(col_at >= NV, col_at - NV, jnp.where(col_at < 0, 0, col_at))
        b_block = (b_at * 5243) >> 17
        g_lane = jnp.full((8, NW), 99, I32)
        for k in range(NB):
            g_lane = jnp.where(b_block == k, virt[k], g_lane)
        g_lane = jnp.where((col_at >= 0) & (col_at < 2 * NV), g_lane, 99)
        for q in range(4):
            want = g_zero ^ g_own ^ virt[4 * r + q]
            masks[p, q] = one(jnp.broadcast_to(g_lane[0:1, :], (32, NW)) == want)

    prow = iota((PR, 128), 0)
    late = prow >= 128
    slot = jnp.where(late, 16 + (prow & 7), prow & 15)
    i_row = jnp.where(late, (prow - 128) >> 3, prow >> 4)
    h_i = jnp.zeros((PR, 128), I32)
    for i in range(PI):
        h_i = jnp.where(i_row == i, occ[i], h_i)
    slot_ok = (jnp.broadcast_to(rank_lane, (PR, 128)) - first_rank) == slot
    pair_class = jnp.broadcast_to(h_row, (PR, 128)) ^ h_i
    s_t = lax.dot_general(
        s_pad, one(iota((32, 128), 0) == (iota((32, 128), 1) & 31)),
        (((0,), (0,)), ((), ())), preferred_element_type=F32,
    ).astype(BF)
    by_class = [
        jnp.dot(
            one(slot_ok & (pair_class == (virt[4 * r + q] ^ g_own))), s_t,
            preferred_element_type=F32,
        )
        for q in range(4)
    ]
    plane = iota((PR, 128), 1)
    for tile in range(KP // 128):
        begin = 8 * (tile % 13) + tile // 13
        low, high = min(3, begin // VB), min(3, (begin + 6) // VB)
        value = by_class[low]
        if low != high:
            value = jnp.where(2 * (plane >> 5) + begin < VB * high, value, by_class[high])
        sjx[:, tile * 128 : tile * 128 + 128] = value
    for p in range(2):
        c_at = 2 * (iota((128, KH), 1) >> 5) + p
        spread_c[:, KH * p : KH * p + KH] = one(iota((128, KH), 0) == c_at)

    erow = iota((32, 128), 0)
    keep = (
        ((h_lane[0:32, :] ^ occ[r]) == (g_zero ^ g_own))
        & (jnp.broadcast_to(rank_lane, (32, 128)) - first_rank == erow)
        & (iota((32, 128), 1) < NOCC)
        & (erow < SLOT)
    )
    expand[...] = one(keep)

    for p in range(2):
        bm[p, 1600:KH, :] = jnp.zeros((KH - 1600, NW), BF)

    def arrange(lo, hi):
        def step(n, carry):
            at = pl.multiple_of(n * 128, 128)
            for p in range(2):
                for q in range(4):
                    ks = [k for k in range(lo, hi) if (2 * k + p) // VB == q]
                    if not ks:
                        continue
                    ok = masks[p, q, 0:VB, pl.ds(at, 128)] > 0
                    for k in ks:
                        from_at = pl.multiple_of(128 * (25 * (k % 10) + 12 * p) + at, 128)
                        v = bv[k // 10, :, pl.ds(from_at, 128)]
                        v = jnp.where(ok, v, jnp.zeros_like(v))
                        bm[p, 32 * k : 32 * k + 32, pl.ds(at, 128)] = pad_rows(v)
            return carry
        lax.fori_loop(0, NW // 128, step, 0)

    for k in range(2):
        int_copy(k).wait()
    arrange(0, 20)

    for k in range(2, BCH):
        int_copy(k).wait()
    arrange(20, 50)

    @pl.when(is_source)
    def _():
        for_targets(lambda copy: copy.wait_send())

    for t in range(4):
        me = at_home & (my_q == t)

        @pl.when(jnp.logical_not(me))
        def _():
            copy_to(partner, s_own, s_in.at[t], ssend.at[t], srecv.at[t]).wait_recv()

        @pl.when(me)
        def _():
            s_in[t] = s_own[...]

    pack = s_in[0].astype(F32)
    for t in range(1, 4):
        pack = pack + s_in[t].astype(F32)
    first = jnp.dot(pack.astype(BF), spread_c[...], preferred_element_type=F32)
    for tile in range(KP // 128):
        cols = slice(tile * 128, tile * 128 + 128)
        for block in range(PR // 16):
            rows = slice(16 * block, 16 * block + 16)
            if block < PI:
                left = jnp.broadcast_to(first[block : block + 1, cols], (16, 128))
            else:
                i = 2 * (block - PI)
                left = jnp.concatenate(
                    [jnp.broadcast_to(first[k : k + 1, cols], (8, 128)) for k in (i, i + 1)],
                    axis=0,
                )
            value = rt[rows, cols].astype(F32) + left * sjx[rows, cols]
            ct[rows, cols] = value.astype(BF)

    def main(lo, hi):
        for p in range(2):
            acc[p, :, lo:hi] = jnp.dot(
                ct[:, KH * p : KH * p + KH], bm[p, :, lo:hi], preferred_element_type=F32
            )

    core_copy = copy_to(partner, core_out, core_in, csend, crecv)

    def xy_copy(k):
        row, col = xy_peer(k)
        src = qb.at[
            pl.ds(pl.multiple_of(16 * row, 16), 16),
            pl.ds(pl.multiple_of(lax.rem(col // 2, 2) * 768, 128), 768),
        ]
        return copy_to((row, col), src, xy_in.at[k - 1], rsend.at[k - 1], rrecv.at[k - 1])

    wide = iota((PR, 128), 1)

    def start_of(a):
        return 0 if a == 0 else 768

    def summed_tile(a, n):
        n = n + start_of(a) // 128
        cols = slice(n * 128, n * 128 + 128)
        value = acc[0, :, cols]
        turned = pltpu.roll(acc[1, :, cols], 64, 1)
        after = 0.0
        if n < NW // 128 - 1:
            after = pltpu.roll(acc[1, :, n * 128 + 128 : n * 128 + 256], 64, 1)
        return value + jnp.where(wide < 64, turned, after)

    def give(a):
        for n in range(7):
            core_out[:, n * 128 : n * 128 + 128] = summed_tile(a, n).astype(BF)
        core_copy.start()

    def keep_own(a):
        for n in range(7):
            psum[:, n * 128 : n * 128 + 128] = summed_tile(a, n)

    def spread(a):
        core_copy.wait_recv()
        total = psum[...] + core_in[...].astype(F32)
        for yh in range(2):
            tiles = []
            for pair in range(4):
                sides = []
                for odd in range(2):
                    begin = NV * a - start_of(a) + 200 * pair + 100 * odd + 50 * yh
                    tile, s = begin // 128, begin % 128
                    by = (64 * odd - s) % 128
                    v = total[:, tile * 128 : tile * 128 + 128]
                    v = pltpu.roll(v, by, 1) if by else v
                    if s + 50 > 128:
                        u = total[:, tile * 128 + 128 : tile * 128 + 256]
                        u = pltpu.roll(u, by, 1) if by else u
                        v = jnp.where(wide < 64 * odd + 128 - s, v, u)
                    sides.append(v)
                v = jnp.where(wide < 64, sides[0], sides[1])
                tiles.append(v)
                cols = slice(yh * 768 + pair * 128, yh * 768 + pair * 128 + 128)
                qf[:, cols] = v[0:128, :]
                qb[:, cols] = v[0:128, :].astype(BF)
            for e in range(2):
                cols = slice(yh * 768 + 512 + e * 128, yh * 768 + 640 + e * 128)
                for i in range(PI):
                    v = jnp.concatenate(
                        [tiles[e + 2 * k][128 + 8 * i : 136 + 8 * i, :] for k in range(2)], axis=0
                    )
                    qf[16 * i : 16 * i + 16, cols] = v
                    qb[16 * i : 16 * i + 16, cols] = v.astype(BF)

        for k in XY_ORDER:
            xy_copy(k).start()

    main(0, 1024)

    @pl.when(core == 1)
    def _():
        give(0)

    @pl.when(core == 0)
    def _():
        keep_own(0)

    main(1024, NW)

    @pl.when(core == 0)
    def _():
        give(1)
        spread(0)

    @pl.when(core == 1)
    def _():
        keep_own(1)
        spread(1)

    total = qf[
        pl.ds(pl.multiple_of(16 * r, 16), 16),
        pl.ds(pl.multiple_of(768 * y_hi, 128), 768),
    ]
    for k in XY_ORDER[::-1]:
        xy_copy(k).wait_recv()
        total = total + xy_in[k - 1].astype(F32)

    def z_copy(k, to_core):
        to = wrap(z + k, 8)
        return copy_to(
            device(x, y, to, to_core), zb.at[to], z_in.at[core, z],
            zsend.at[to_core, k], zrecv.at[core, z],
        )

    zlane = iota((16, 128), 1)
    zsub = iota((16, 128), 0)
    for to in range(8):
        pair, odd = to // 2, to % 2
        early = total[:, pair * 128 : pair * 128 + 128]
        late8 = total[:, 512 + (pair % 2) * 128 : 640 + (pair % 2) * 128]
        if pair // 2:
            late8 = jnp.concatenate([late8[8:16, :], late8[0:8, :]], axis=0)
        if odd:
            early = pltpu.roll(early, 64, 1)
        else:
            late8 = pltpu.roll(late8, 64, 1)
        part = jnp.where(zlane < 64, early, jnp.where(zsub < 8, late8, 0.0))
        zf[to] = part
        zb[to] = part.astype(BF)
    for k in Z_ORDER:
        for to_core in range(2):
            z_copy(k, to_core).start()
    partner_copy = copy_to(
        partner, zb.at[z], z_in.at[core, z], zsend.at[0, 0], zrecv.at[core, z]
    )
    partner_copy.start()

    core_copy.wait_send()
    for k in range(1, 16):
        xy_copy(k).wait_send()
    partner_copy.wait_send()
    copy_to(
        partner, zb.at[z], z_in.at[1 - core, z], zsend.at[0, 0], zrecv.at[1 - core, z]
    ).wait_recv()
    own, other = zf[z], z_in[1 - core, z].astype(F32)
    sums = [jnp.where(core == a, own, other) for a in range(2)]
    for k in Z_ORDER[::-1]:
        origin = wrap(z + (8 - k), 8)
        for a in range(2):
            z_copy(k, a).wait_send()
            copy_to(
                partner, zb.at[z], z_in.at[a, origin], zsend.at[a, k], zrecv.at[a, origin]
            ).wait_recv()
            sums[a] = sums[a] + z_in[a, origin].astype(F32)
    sums = [v.astype(BF) for v in sums]

    osub = iota((64, 128), 0)
    b_own = osub & 31
    wanted = ((osub >> 5) << 6) + core * VB + b_own
    select = one((iota((64, 128), 1) == wanted) & (b_own < VB))
    for a in range(2):
        narrow = lax.dot_general(
            select, sums[a], (((1,), (1,)), ((), ())), preferred_element_type=F32
        ).astype(BF)
        final = jnp.dot(narrow[0:32, :], expand[0:16, :], preferred_element_type=F32)
        final = final + jnp.dot(narrow[32:64, :], expand[16:32, :], preferred_element_type=F32)
        out[a] = final.astype(BF)[0:VB, 0:NOCC]


def run_round(index, amplitudes, singles_t, integrals, virt_irrep, occ_irrep):
    smem = pl.BlockSpec(memory_space=pltpu.SMEM)
    vmem = pl.BlockSpec(memory_space=pltpu.VMEM)
    hbm = pl.BlockSpec(memory_space=pl.ANY)
    dma = pltpu.SemaphoreType.DMA
    return pl.pallas_call(
        kernel,
        out_shape=(
            jax.ShapeDtypeStruct((2, VB, NOCC), BF),
            jax.ShapeDtypeStruct((1,), I32),
        ),
        in_specs=[smem, smem, smem, vmem, vmem, hbm, hbm],
        out_specs=(vmem, smem),
        scratch_shapes=[
            pltpu.VMEM((4, VB, ALEN), BF),
            pltpu.VMEM((BCH, VB, BLEN), BF),
            pltpu.VMEM((992, 128), I32),
            pltpu.VMEM((4, 992, 256), BF),
            pltpu.VMEM((KP, 256), BF),
            pltpu.VMEM((PR, KP), BF),
            pltpu.VMEM((PR, KP), BF),
            pltpu.VMEM((2, 4, 32, NW), BF),
            pltpu.VMEM((2, KH, NW), BF),
            pltpu.VMEM((PR, KP), F32),
            pltpu.VMEM((128, KP), BF),
            pltpu.VMEM((2, PR, NW), F32),
            pltpu.VMEM((PR, 896), F32),
            pltpu.VMEM((16, 128), BF),
            pltpu.VMEM((4, 16, 128), BF),
            pltpu.VMEM((32, 128), BF),
            pltpu.VMEM((PR, 896), BF),
            pltpu.VMEM((PR, 896), BF),
            pltpu.VMEM((128, 1536), F32),
            pltpu.VMEM((128, 1536), BF),
            pltpu.VMEM((15, 16, 768), BF),
            pltpu.VMEM((8, 16, 128), F32),
            pltpu.VMEM((8, 16, 128), BF),
            pltpu.VMEM((2, 8, 16, 128), BF),
            dma((4,)), dma((BCH,)), dma((16,)), dma((4,)), dma, dma,
            dma((15,)), dma((15,)), dma((2, 8)), dma((2, 8)),
        ],
        compiler_params=pltpu.CompilerParams(
            collective_id=0, has_side_effects=True, vmem_limit_bytes=58 * 1024 * 1024
        ),
        name="ladder_round",
    )(
        index, virt_irrep, occ_irrep, occ_irrep.reshape(1, NOCC), singles_t,
        amplitudes, integrals,
    )


def body(amplitudes, singles, integrals, virt_irrep, occ_irrep):
    singles_t = jnp.transpose(singles)

    def more(state):
        return state[0] < state[1][0]

    def step(state):
        index, _, total = state
        part, rounds = run_round(
            jnp.full((1,), index, I32), amplitudes, singles_t, integrals, virt_irrep, occ_irrep
        )
        return index + 1, rounds, total + part

    start = (jnp.int32(0), jnp.ones((1,), I32), jnp.zeros((2, VB, NOCC), BF))
    _, _, total = lax.while_loop(more, step, start)
    return jnp.transpose(total, (2, 0, 1))


def solution(mesh):
    placed = (P("col", "row"), P(None, "col"), P("col", "row"), P(), P())
    return jax.shard_map(
        body, mesh=mesh, in_specs=placed, out_specs=P("row", None, "col"), check_vma=False
    )
```

```python
import functools

import jax
import jax.numpy as jnp
from jax import lax
from jax.experimental import pallas as pl
from jax.experimental.pallas import tpu as pltpu
from jax.sharding import PartitionSpec as P

MESH = pl.DeviceIdType.MESH
BF = jnp.bfloat16
F32 = jnp.float32
I32 = jnp.int32

VB = 25
NB = 32
NOCC = 100
PI = 8
ROWS, COLS = 8, 32
NC = 100
SLOT = 24
PR = PI * SLOT
WIN = 896
ALEN = 157 * 128
KP = 3328
KH = KP // 2
BCH = 5
BLEN = 20 * 1600
NW = 13 * 128
NV = 800
Z_ORDER = (4, 3, 5, 2, 6, 1, 7)
XY_ORDER = (10, 6, 9, 11, 14, 2, 5, 7, 8, 13, 15, 1, 3, 4, 12)


def iota(shape, dim):
    return lax.broadcasted_iota(I32, shape, dim)


def pad_rows(x):
    return jnp.concatenate([x, jnp.zeros((32 - x.shape[0], x.shape[1]), x.dtype)], axis=0)


def one(cond):
    return jnp.where(cond, 1.0, 0.0).astype(BF)


def kernel(
    round_ref, virt, occ, occ_row, singles, amp, integ,
    out, rounds_out,
    av, bv, enc, onehot, cs, rt, ct, masks, bm, sjx, spread_c, acc, psum, s_own, s_in, expand,
    core_out, core_in, qf, qb, xy_in, zf, zb, z_in,
    asem, bsem, ssend, srecv, csend, crecv, rsend, rrecv, zsend, zrecv,
):
    r = lax.axis_index("row")
    c = lax.axis_index("col")
    x = lax.rem(r, 4)
    y_lo = r // 4
    z = c // 4
    y_hi = lax.rem(c // 2, 2)
    core = lax.rem(c, 2)
    y = 2 * y_hi + y_lo

    def device(x, y, z, core):
        return lax.rem(y, 2) * 4 + x, z * 4 + (y // 2) * 2 + core

    def copy_to(where, src, dst, send, recv):
        return pltpu.make_async_remote_copy(
            src_ref=src, dst_ref=dst, send_sem=send, recv_sem=recv,
            device_id=where, device_id_type=MESH,
        )

    barrier = pltpu.get_barrier_semaphore()
    at_home = r == z
    is_source = x == lax.rem(z, 4)
    target_y = jnp.where(y_lo == z // 4, y, 3 - y)

    def greet(where):
        pl.semaphore_signal(barrier, inc=1, device_id=where, device_id_type=MESH)

    def wrap(v, n):
        return jnp.where(v >= n, v - n, v)

    def z_peer(k, to_core):
        return device(x, y, wrap(z + k, 8), to_core)

    def xy_peer(k):
        return device(wrap(x + k % 4, 4), wrap(y + k // 4, 4), z, core)

    partner = device(x, y, z, 1 - core)

    for sc in range(2):
        greet(device(x, 3 - y, r, sc))
    for sc in range(2):
        @pl.when(jnp.logical_not(at_home & (sc == core)))
        def _():
            greet(device(x, y, r, sc))
    def amp_copy(q):
        return pltpu.make_async_copy(
            amp.at[:, pl.ds(pl.multiple_of(q * (156 * 128), 128), ALEN)], av.at[q], asem.at[q]
        )

    def int_copy(k):
        return pltpu.make_async_copy(
            integ.at[:, pl.ds(pl.multiple_of(k * BLEN, 128), BLEN)], bv.at[k], bsem.at[k]
        )

    for q in range(4):
        amp_copy(q).start()
    for k in range(BCH):
        int_copy(k).start()

    for k in Z_ORDER:
        for sc in range(2):
            greet(z_peer(k, sc))
    for k in XY_ORDER:
        greet(xy_peer(k))
    greet(partner)

    first_rank = round_ref[0] * SLOT
    lane = iota((128, 128), 1)
    sub = iota((128, 128), 0)
    h_row = jnp.concatenate([occ_row[...], jnp.full((1, 128 - NOCC), 99, I32)], axis=1)
    h_lane = jnp.broadcast_to(h_row, (128, 128))
    h_sub = h_lane.T
    same = h_lane == h_sub
    rank_sub = jnp.broadcast_to(
        jnp.sum(jnp.where(same & (lane < sub), 1.0, 0.0), axis=1, keepdims=True).astype(I32),
        (128, 128),
    )
    rank_lane = jnp.sum(
        jnp.where(same & (sub < lane), 1.0, 0.0), axis=0, keepdims=True
    ).astype(I32)
    top = jnp.max(jnp.where(sub < NOCC, rank_sub, 0))
    rounds_out[0] = sum((top >= SLOT * k).astype(I32) for k in range(5))
    rk = rank_sub - first_rank
    fits = (rk >= 0) & (rk < SLOT) & (sub < NOCC)
    enc[pl.ds(0, 96), :] = jnp.full((96, 128), -1, I32)
    enc[pl.ds(896, 96), :] = jnp.full((96, 128), -1, I32)
    for i in range(PI):
        code = jnp.where(rk < 16, rk + 16 * i, rk + (112 + 8 * i))
        value = jnp.where(fits, ((h_sub ^ occ[i]) << 10) + code, -1)
        enc[pl.ds(96 + 100 * i, 100), :] = value[0:100, :]

    g_own = virt[c]
    g_zero = virt[0]

    def build(step, carry):
        q = step // 2
        start = pl.multiple_of(lax.rem(step, 2) * 496, 16)
        kq = virt[4 * r + q] ^ g_own
        e = enc[pl.ds(start, 496), :]
        l2 = iota((496, 128), 1) + (kq << 10)
        onehot[q, pl.ds(start, 496), 0:128] = one(e == l2)
        onehot[q, pl.ds(start, 496), 128:256] = one(e == l2 + 128)
        return carry

    lax.fori_loop(0, 8, build, 0)

    my_q = lax.rem(c, 4)
    s_pad = pad_rows(
        jnp.concatenate([singles[...], jnp.zeros((VB, 128 - NOCC), BF)], axis=1)
    )
    place = one(iota((32, 128), 1) == iota((32, 128), 0) + VB * my_q)
    place = jnp.where(iota((32, 128), 0) < VB, place.astype(F32), 0.0).astype(BF)
    s_own[...] = lax.dot_general(
        s_pad[:, 0:16], place, (((0,), (0,)), ((), ())), preferred_element_type=F32
    ).astype(BF)

    for p in range(2):
        cs[KH * p + 1600 : KH * p + KH, :] = jnp.zeros((KH - 1600, 256), BF)

    def compact(q, carry):
        amp_copy(q).wait()
        for u0 in range(4):
            count = 7 if u0 == 0 else 6
            step = (q + u0) // 4
            pieces = []
            for w in range(count):
                base = pl.multiple_of(128 * (25 * w + 6 * u0 + step), 128)
                pieces.append(pad_rows(av[q, :, pl.ds(base, WIN)]))
            left = jnp.concatenate(pieces, axis=0)
            start = pl.multiple_of(96 - 32 * lax.rem(q + u0, 4), 32)
            got = jnp.dot(
                left, onehot[q, pl.ds(start, WIN), :], preferred_element_type=F32
            ).astype(BF)
            at0 = KH * lax.rem(q + u0, 2) + 32 * ((25 * q + u0) // 2)
            for w in range(count):
                at = pl.multiple_of(at0 + 64 * w, 32)
                cs[pl.ds(at, 32), :] = got[32 * w : 32 * w + 32, :]
        return carry

    lax.fori_loop(0, 4, compact, 0)

    pl.semaphore_wait(
        barrier,
        30 + jnp.where(is_source, 16, 0) - jnp.where(is_source & at_home, 1, 0),
    )

    def singles_copy(k, tc):
        return copy_to(
            device(x, target_y, wrap(z + k, 8), tc), s_own, s_in.at[my_q],
            ssend.at[2 * k + tc], srecv.at[my_q],
        )

    def for_targets(act):
        for k in Z_ORDER:
            for tc in range(2):
                act(singles_copy(k, tc))
        for tc in range(2):
            @pl.when(jnp.logical_not(at_home & (tc == core)))
            def _():
                act(singles_copy(0, tc))

    @pl.when(is_source)
    def _():
        for_targets(lambda copy: copy.start())

    def turn(step, carry):
        at = pl.multiple_of(step * 256, 256)
        rt[:, pl.ds(at, 256)] = cs[pl.ds(at, 256), :].T[0:PR, :]
        return carry

    lax.fori_loop(0, KP // 256, turn, 0)

    for p in range(2):
        col_at = iota((8, NW), 1) - 64 * p
        b_at = jnp.where(col_at >= NV, col_at - NV, jnp.where(col_at < 0, 0, col_at))
        b_block = (b_at * 5243) >> 17
        g_lane = jnp.full((8, NW), 99, I32)
        for k in range(NB):
            g_lane = jnp.where(b_block == k, virt[k], g_lane)
        g_lane = jnp.where((col_at >= 0) & (col_at < 2 * NV), g_lane, 99)
        for q in range(4):
            want = g_zero ^ g_own ^ virt[4 * r + q]
            masks[p, q] = one(jnp.broadcast_to(g_lane[0:1, :], (32, NW)) == want)

    prow = iota((PR, 128), 0)
    late = prow >= 128
    slot = jnp.where(late, 16 + (prow & 7), prow & 15)
    i_row = jnp.where(late, (prow - 128) >> 3, prow >> 4)
    h_i = jnp.zeros((PR, 128), I32)
    for i in range(PI):
        h_i = jnp.where(i_row == i, occ[i], h_i)
    slot_ok = (jnp.broadcast_to(rank_lane, (PR, 128)) - first_rank) == slot
    pair_class = jnp.broadcast_to(h_row, (PR, 128)) ^ h_i
    s_t = lax.dot_general(
        s_pad, one(iota((32, 128), 0) == (iota((32, 128), 1) & 31)),
        (((0,), (0,)), ((), ())), preferred_element_type=F32,
    ).astype(BF)
    by_class = [
        jnp.dot(
            one(slot_ok & (pair_class == (virt[4 * r + q] ^ g_own))), s_t,
            preferred_element_type=F32,
        )
        for q in range(4)
    ]
    plane = iota((PR, 128), 1)
    for tile in range(KP // 128):
        begin = 8 * (tile % 13) + tile // 13
        low, high = min(3, begin // VB), min(3, (begin + 6) // VB)
        value = by_class[low]
        if low != high:
            value = jnp.where(2 * (plane >> 5) + begin < VB * high, value, by_class[high])
        sjx[:, tile * 128 : tile * 128 + 128] = value
    for p in range(2):
        c_at = 2 * (iota((128, KH), 1) >> 5) + p
        spread_c[:, KH * p : KH * p + KH] = one(iota((128, KH), 0) == c_at)

    erow = iota((32, 128), 0)
    keep = (
        ((h_lane[0:32, :] ^ occ[r]) == (g_zero ^ g_own))
        & (jnp.broadcast_to(rank_lane, (32, 128)) - first_rank == erow)
        & (iota((32, 128), 1) < NOCC)
        & (erow < SLOT)
    )
    expand[...] = one(keep)

    for p in range(2):
        bm[p, 1600:KH, :] = jnp.zeros((KH - 1600, NW), BF)

    def arrange(lo, hi):
        def step(n, carry):
            at = pl.multiple_of(n * 128, 128)
            for p in range(2):
                for q in range(4):
                    ks = [k for k in range(lo, hi) if (2 * k + p) // VB == q]
                    if not ks:
                        continue
                    ok = masks[p, q, 0:VB, pl.ds(at, 128)] > 0
                    for k in ks:
                        from_at = pl.multiple_of(128 * (25 * (k % 10) + 12 * p) + at, 128)
                        v = bv[k // 10, :, pl.ds(from_at, 128)]
                        v = jnp.where(ok, v, jnp.zeros_like(v))
                        bm[p, 32 * k : 32 * k + 32, pl.ds(at, 128)] = pad_rows(v)
            return carry
        lax.fori_loop(0, NW // 128, step, 0)

    for k in range(2):
        int_copy(k).wait()
    arrange(0, 20)

    for k in range(2, BCH):
        int_copy(k).wait()
    arrange(20, 50)

    @pl.when(is_source)
    def _():
        for_targets(lambda copy: copy.wait_send())

    for t in range(4):
        me = at_home & (my_q == t)

        @pl.when(jnp.logical_not(me))
        def _():
            copy_to(partner, s_own, s_in.at[t], ssend.at[t], srecv.at[t]).wait_recv()

        @pl.when(me)
        def _():
            s_in[t] = s_own[...]

    pack = s_in[0].astype(F32)
    for t in range(1, 4):
        pack = pack + s_in[t].astype(F32)
    first = jnp.dot(pack.astype(BF), spread_c[...], preferred_element_type=F32)
    for tile in range(KP // 128):
        cols = slice(tile * 128, tile * 128 + 128)
        for block in range(PR // 16):
            rows = slice(16 * block, 16 * block + 16)
            if block < PI:
                left = jnp.broadcast_to(first[block : block + 1, cols], (16, 128))
            else:
                i = 2 * (block - PI)
                left = jnp.concatenate(
                    [jnp.broadcast_to(first[k : k + 1, cols], (8, 128)) for k in (i, i + 1)],
                    axis=0,
                )
            value = rt[rows, cols].astype(F32) + left * sjx[rows, cols]
            ct[rows, cols] = value.astype(BF)

    def main(lo, hi):
        for p in range(2):
            acc[p, :, lo:hi] = jnp.dot(
                ct[:, KH * p : KH * p + KH], bm[p, :, lo:hi], preferred_element_type=F32
            )

    core_copy = copy_to(partner, core_out, core_in, csend, crecv)

    def xy_copy(k):
        row, col = xy_peer(k)
        src = qb.at[
            pl.ds(pl.multiple_of(16 * row, 16), 16),
            pl.ds(pl.multiple_of(lax.rem(col // 2, 2) * 768, 128), 768),
        ]
        return copy_to((row, col), src, xy_in.at[k - 1], rsend.at[k - 1], rrecv.at[k - 1])

    wide = iota((PR, 128), 1)

    def start_of(a):
        return 0 if a == 0 else 768

    def summed_tile(a, n):
        n = n + start_of(a) // 128
        cols = slice(n * 128, n * 128 + 128)
        value = acc[0, :, cols]
        turned = pltpu.roll(acc[1, :, cols], 64, 1)
        after = 0.0
        if n < NW // 128 - 1:
            after = pltpu.roll(acc[1, :, n * 128 + 128 : n * 128 + 256], 64, 1)
        return value + jnp.where(wide < 64, turned, after)

    def give(a):
        for n in range(7):
            core_out[:, n * 128 : n * 128 + 128] = summed_tile(a, n).astype(BF)
        core_copy.start()

    def keep_own(a):
        for n in range(7):
            psum[:, n * 128 : n * 128 + 128] = summed_tile(a, n)

    def spread(a):
        core_copy.wait_recv()
        total = psum[...] + core_in[...].astype(F32)
        for yh in range(2):
            tiles = []
            for pair in range(4):
                sides = []
                for odd in range(2):
                    begin = NV * a - start_of(a) + 200 * pair + 100 * odd + 50 * yh
                    tile, s = begin // 128, begin % 128
                    by = (64 * odd - s) % 128
                    v = total[:, tile * 128 : tile * 128 + 128]
                    v = pltpu.roll(v, by, 1) if by else v
                    if s + 50 > 128:
                        u = total[:, tile * 128 + 128 : tile * 128 + 256]
                        u = pltpu.roll(u, by, 1) if by else u
                        v = jnp.where(wide < 64 * odd + 128 - s, v, u)
                    sides.append(v)
                v = jnp.where(wide < 64, sides[0], sides[1])
                tiles.append(v)
                cols = slice(yh * 768 + pair * 128, yh * 768 + pair * 128 + 128)
                qf[:, cols] = v[0:128, :]
                qb[:, cols] = v[0:128, :].astype(BF)
            for e in range(2):
                cols = slice(yh * 768 + 512 + e * 128, yh * 768 + 640 + e * 128)
                for i in range(PI):
                    v = jnp.concatenate(
                        [tiles[e + 2 * k][128 + 8 * i : 136 + 8 * i, :] for k in range(2)], axis=0
                    )
                    qf[16 * i : 16 * i + 16, cols] = v
                    qb[16 * i : 16 * i + 16, cols] = v.astype(BF)

        for k in XY_ORDER:
            xy_copy(k).start()

    main(0, 1024)

    @pl.when(core == 1)
    def _():
        give(0)

    @pl.when(core == 0)
    def _():
        keep_own(0)

    main(1024, NW)

    @pl.when(core == 0)
    def _():
        give(1)
        spread(0)

    @pl.when(core == 1)
    def _():
        keep_own(1)
        spread(1)

    total = qf[
        pl.ds(pl.multiple_of(16 * r, 16), 16),
        pl.ds(pl.multiple_of(768 * y_hi, 128), 768),
    ]
    for k in XY_ORDER[::-1]:
        xy_copy(k).wait_recv()
        total = total + xy_in[k - 1].astype(F32)

    def z_copy(k, to_core):
        to = wrap(z + k, 8)
        return copy_to(
            device(x, y, to, to_core), zb.at[to], z_in.at[core, z],
            zsend.at[to_core, k], zrecv.at[core, z],
        )

    zlane = iota((16, 128), 1)
    zsub = iota((16, 128), 0)
    for to in range(8):
        pair, odd = to // 2, to % 2
        early = total[:, pair * 128 : pair * 128 + 128]
        late8 = total[:, 512 + (pair % 2) * 128 : 640 + (pair % 2) * 128]
        if pair // 2:
            late8 = jnp.concatenate([late8[8:16, :], late8[0:8, :]], axis=0)
        if odd:
            early = pltpu.roll(early, 64, 1)
        else:
            late8 = pltpu.roll(late8, 64, 1)
        part = jnp.where(zlane < 64, early, jnp.where(zsub < 8, late8, 0.0))
        zf[to] = part
        zb[to] = part.astype(BF)
    for k in Z_ORDER:
        for to_core in range(2):
            z_copy(k, to_core).start()
    partner_copy = copy_to(
        partner, zb.at[z], z_in.at[core, z], zsend.at[0, 0], zrecv.at[core, z]
    )
    partner_copy.start()

    core_copy.wait_send()
    for k in range(1, 16):
        xy_copy(k).wait_send()
    partner_copy.wait_send()
    copy_to(
        partner, zb.at[z], z_in.at[1 - core, z], zsend.at[0, 0], zrecv.at[1 - core, z]
    ).wait_recv()
    own, other = zf[z], z_in[1 - core, z].astype(F32)
    sums = [jnp.where(core == a, own, other) for a in range(2)]
    for k in Z_ORDER[::-1]:
        origin = wrap(z + (8 - k), 8)
        for a in range(2):
            z_copy(k, a).wait_send()
            copy_to(
                partner, zb.at[z], z_in.at[a, origin], zsend.at[a, k], zrecv.at[a, origin]
            ).wait_recv()
            sums[a] = sums[a] + z_in[a, origin].astype(F32)
    sums = [v.astype(BF) for v in sums]

    osub = iota((64, 128), 0)
    b_own = osub & 31
    wanted = ((osub >> 5) << 6) + core * VB + b_own
    select = one((iota((64, 128), 1) == wanted) & (b_own < VB))
    for a in range(2):
        narrow = lax.dot_general(
            select, sums[a], (((1,), (1,)), ((), ())), preferred_element_type=F32
        ).astype(BF)
        final = jnp.dot(narrow[0:32, :], expand[0:16, :], preferred_element_type=F32)
        final = final + jnp.dot(narrow[32:64, :], expand[16:32, :], preferred_element_type=F32)
        out[a] = final.astype(BF)[0:VB, 0:NOCC]


def run_round(index, amplitudes, singles_t, integrals, virt_irrep, occ_irrep):
    smem = pl.BlockSpec(memory_space=pltpu.SMEM)
    vmem = pl.BlockSpec(memory_space=pltpu.VMEM)
    hbm = pl.BlockSpec(memory_space=pl.ANY)
    dma = pltpu.SemaphoreType.DMA
    return pl.pallas_call(
        kernel,
        out_shape=(
            jax.ShapeDtypeStruct((2, VB, NOCC), BF),
            jax.ShapeDtypeStruct((1,), I32),
        ),
        in_specs=[smem, smem, smem, vmem, vmem, hbm, hbm],
        out_specs=(vmem, smem),
        scratch_shapes=[
            pltpu.VMEM((4, VB, ALEN), BF),
            pltpu.VMEM((BCH, VB, BLEN), BF),
            pltpu.VMEM((992, 128), I32),
            pltpu.VMEM((4, 992, 256), BF),
            pltpu.VMEM((KP, 256), BF),
            pltpu.VMEM((PR, KP), BF),
            pltpu.VMEM((PR, KP), BF),
            pltpu.VMEM((2, 4, 32, NW), BF),
            pltpu.VMEM((2, KH, NW), BF),
            pltpu.VMEM((PR, KP), F32),
            pltpu.VMEM((128, KP), BF),
            pltpu.VMEM((2, PR, NW), F32),
            pltpu.VMEM((PR, 896), F32),
            pltpu.VMEM((16, 128), BF),
            pltpu.VMEM((4, 16, 128), BF),
            pltpu.VMEM((32, 128), BF),
            pltpu.VMEM((PR, 896), BF),
            pltpu.VMEM((PR, 896), BF),
            pltpu.VMEM((128, 1536), F32),
            pltpu.VMEM((128, 1536), BF),
            pltpu.VMEM((15, 16, 768), BF),
            pltpu.VMEM((8, 16, 128), F32),
            pltpu.VMEM((8, 16, 128), BF),
            pltpu.VMEM((2, 8, 16, 128), BF),
            dma((4,)), dma((BCH,)), dma((16,)), dma((4,)), dma, dma,
            dma((15,)), dma((15,)), dma((2, 8)), dma((2, 8)),
        ],
        compiler_params=pltpu.CompilerParams(
            collective_id=0, has_side_effects=True, vmem_limit_bytes=58 * 1024 * 1024
        ),
        name="ladder_round",
    )(
        index, virt_irrep, occ_irrep, occ_irrep.reshape(1, NOCC), singles_t,
        amplitudes, integrals,
    )


def body(amplitudes, singles, integrals, virt_irrep, occ_irrep):
    singles_t = jnp.transpose(singles)

    def more(state):
        return state[0] < state[1][0]

    def step(state):
        index, _, total = state
        part, rounds = run_round(
            jnp.full((1,), index, I32), amplitudes, singles_t, integrals, virt_irrep, occ_irrep
        )
        return index + 1, rounds, total + part

    start = (jnp.int32(0), jnp.ones((1,), I32), jnp.zeros((2, VB, NOCC), BF))
    _, _, total = lax.while_loop(more, step, start)
    return jnp.transpose(total, (2, 0, 1))


def solution(mesh):
    placed = (P("col", "row"), P(None, "col"), P("col", "row"), P(), P())
    return jax.shard_map(
        body, mesh=mesh, in_specs=placed, out_specs=P("row", None, "col"), check_vma=False
    )
```
